32 devices in a mesh: ctx: 8 (over y, x, core), head: 4 (over z).
Axes of the slice: x: 2, y: 2, z: 4, core: 2. Of those that a mesh axis runs over, the one named last changes fastest.
Arguments:
- queries: bfloat16 [1024, 12288], P('ctx', 'head'), may hold values from -8 to 8
- latents: bfloat16 [1024, 512], P('ctx'), may hold values from -4 to 4
- rope_key: bfloat16 [1024, 64], P('ctx'), may hold values from -8 to 8
- up_key_weight: bfloat16 [512, 8192], P(None, 'head'), may hold values from -0.5 to 0.5
- up_value_weight: bfloat16 [512, 8192], P(None, 'head'), may hold values from -0.25 to 0.25
- out_grad: bfloat16 [1024, 8192], P('ctx', 'head'), may hold values from -6 to 6
- group_order: int32 [16], replicated, may hold values from 0 to 15, as said below
Outputs:
- query_grad: bfloat16 [1024, 12288], P('ctx', 'head')
- latent_grad: float32 [1024, 512], P('ctx')
- rope_grad: float32 [1024, 64], P('ctx')
- up_key_grad: float32 [512, 8192], P('ctx', 'head')
- up_value_grad: float32 [512, 8192], P('ctx', 'head')
The draws below stay inside these ranges and needn't reach their ends.
Inputs may be any that keep to these rules, and one draw needn't show every extreme that they name: A permutation of the 16 group numbers; storage slot k (rows k * 64 to k * 64 + 63) holds the sequence positions group_order[k] * 64 on, in order.
All inputs are finite; a program needn't handle non-finite values.
Results may differ from the reference program's by a relative error of at most 0.017.
Values may be sent and summed in bfloat16 or wider, within the bound.
A program may use at most 64 MiB of HBM per device.

```python
import jax
import jax.numpy as jnp
from jax import lax

D_LATENT = 512
ROPE = 64
NOPE = 128
VDIM = 128
HEADS = 64
TOKENS = 1024
GROUP = 64
GROUPS = 16


def draw_rope_key(key, part):
    values = jax.random.normal(jax.random.fold_in(key, 5), (TOKENS, ROPE), jnp.float32)
    return jnp.clip(values, -8.0, 8.0).astype(jnp.bfloat16)


def draw_queries(key, part):
    values = jax.random.normal(jax.random.fold_in(key, 9), (TOKENS, HEADS * (NOPE + ROPE)), jnp.float32)
    return jnp.clip(values, -8.0, 8.0).astype(jnp.bfloat16)


def draw_group_order(key, part):
    return jax.random.permutation(jax.random.fold_in(key, 3), GROUPS).astype(jnp.int32)


def shard_levels(stream_key, shape, shards, low, largest):
    factor_of, own = 1.0, jax.random.fold_in(stream_key, 6)
    for dim, parts in shards:
        heights = jnp.exp(jax.random.uniform(jax.random.fold_in(own, dim), (parts,), jnp.float32, low / len(shards), largest / len(shards)))
        factor_of = factor_of * jnp.repeat(heights, shape[dim] // parts).reshape([-1 if axis == dim else 1 for axis in range(len(shape))])
    return factor_of


def normal_values(stream_key, shape, scale, bound, pieces=(), kind=jnp.bfloat16):
    drawn = jax.random.normal(stream_key, shape, jnp.float32) * scale
    if len(pieces) > 0:
        drawn = shard_levels(stream_key, shape, pieces, -0.22, 0.18) * drawn
    return jnp.clip(drawn, min=-bound, max=bound).astype(kind)


def setup_inputs(seed: int = 0) -> dict:
    seeds = jax.random.split(jax.random.key(seed), 8)
    return {
        "queries": draw_queries(jax.random.fold_in(seeds[7], 71), 0),
        "latents": normal_values(seeds[1], (TOKENS, D_LATENT), 0.5, 4.0, ((0, 8),)),
        "rope_key": draw_rope_key(jax.random.fold_in(seeds[7], 71), 0),
        "up_key_weight": normal_values(seeds[3], (D_LATENT, HEADS * NOPE), NOPE ** -0.5, 0.5, ((1, 4),)),
        "up_value_weight": normal_values(seeds[4], (D_LATENT, HEADS * VDIM), D_LATENT ** -0.5, 0.25, ((1, 4),)),
        "out_grad": normal_values(seeds[5], (TOKENS, HEADS * VDIM), 1.0, 6.0, ((0, 8), (1, 4))),
        "group_order": draw_group_order(jax.random.fold_in(seeds[7], 71), 0),
    }


NEG_FILL = -1.0e30


def reference(queries, latents, rope_key, up_key_weight, up_value_weight, out_grad, group_order):
    scale_factor = (NOPE + ROPE) ** -0.5
    head_width = NOPE + ROPE
    row_ids = jnp.arange(TOKENS, dtype=jnp.int32)
    positions = group_order[row_ids // GROUP] * GROUP + row_ids % GROUP
    visible = positions[None, :] <= positions[:, None]

    def one_head(carried, head_index):
        all_latent, all_rope = carried
        query_head = lax.dynamic_slice_in_dim(queries, head_index * head_width, head_width, 1)
        query_nope = query_head[:, :NOPE]
        query_rope = query_head[:, NOPE:]
        up_key = lax.dynamic_slice_in_dim(up_key_weight, head_index * NOPE, NOPE, 1)
        up_value = lax.dynamic_slice_in_dim(up_value_weight, head_index * VDIM, VDIM, 1)
        grad_head = lax.dynamic_slice_in_dim(out_grad, head_index * VDIM, VDIM, 1)
        query_abs = jnp.dot(query_nope, up_key.T, preferred_element_type=jnp.float32).astype(jnp.bfloat16)
        grad_lat = jnp.dot(grad_head, up_value.T, preferred_element_type=jnp.float32).astype(jnp.bfloat16)
        scores = (jnp.dot(query_abs, latents.T, preferred_element_type=jnp.float32)
                  + jnp.dot(query_rope, rope_key.T, preferred_element_type=jnp.float32)) * scale_factor
        row_max = jnp.max(jnp.where(visible, scores, NEG_FILL), axis=1, keepdims=True)
        log_total = row_max + jnp.log(jnp.sum(jnp.where(visible, jnp.exp(scores - row_max), 0.0), axis=1, keepdims=True))
        softmax_rows = jnp.where(visible, jnp.exp(scores - log_total), 0.0)
        grad_prob = jnp.dot(grad_lat, latents.T, preferred_element_type=jnp.float32)
        row_delta = jnp.sum(softmax_rows * grad_prob, axis=1, keepdims=True)
        grad_score = softmax_rows * (grad_prob - row_delta) * scale_factor
        probs_low = softmax_rows.astype(jnp.bfloat16)
        grad_low = grad_score.astype(jnp.bfloat16)
        out_latent = jnp.dot(probs_low, latents, preferred_element_type=jnp.float32).astype(jnp.bfloat16)
        grad_abs = jnp.dot(grad_low, latents, preferred_element_type=jnp.float32).astype(jnp.bfloat16)
        grad_nope = jnp.dot(grad_abs, up_key, preferred_element_type=jnp.float32)
        grad_rope = jnp.dot(grad_low, rope_key, preferred_element_type=jnp.float32)
        query_part = jnp.concatenate([grad_nope, grad_rope], axis=1).astype(jnp.bfloat16)
        latent_part = (jnp.dot(grad_low.T, query_abs, preferred_element_type=jnp.float32)
                       + jnp.dot(probs_low.T, grad_lat, preferred_element_type=jnp.float32))
        rope_part = jnp.dot(grad_low.T, query_rope, preferred_element_type=jnp.float32)
        key_part = jnp.dot(grad_abs.T, query_nope, preferred_element_type=jnp.float32)
        value_part = jnp.dot(out_latent.T, grad_head, preferred_element_type=jnp.float32)
        return (all_latent + latent_part, all_rope + rope_part), (query_part, key_part, value_part)

    initial = (jnp.zeros((TOKENS, D_LATENT), jnp.float32), jnp.zeros((TOKENS, ROPE), jnp.float32))
    sums, stacked = lax.scan(one_head, initial, jnp.arange(HEADS, dtype=jnp.int32))
    latent_grad, rope_grad = sums
    query_parts, key_parts, value_parts = stacked
    query_grad = jnp.transpose(query_parts, (1, 0, 2)).reshape(TOKENS, HEADS * head_width)
    up_key_grad = jnp.transpose(key_parts, (1, 0, 2)).reshape(D_LATENT, HEADS * NOPE)
    up_value_grad = jnp.transpose(value_parts, (1, 0, 2)).reshape(D_LATENT, HEADS * VDIM)
    return query_grad, latent_grad, rope_grad, up_key_grad, up_value_grad
```

```python
import functools

import jax
import jax.numpy as jnp
from jax import lax
from jax.experimental import pallas as pl
from jax.experimental.pallas import tpu as pltpu
from jax.sharding import PartitionSpec as P

D_LATENT = 512
ROPE = 64
NOPE = 128
VDIM = 128
WIDE = 640

NEG_FILL = -1e30
MESH = pl.DeviceIdType.MESH
F32 = jnp.float32
BF16 = jnp.bfloat16


def dot(a, b, ca=1, cb=0):
    return lax.dot_general(a, b, (((ca,), (cb,)), ((), ())), preferred_element_type=F32)


def kernel(
    n, nz, lat_ref, rope_ref, order_ref, q_hbm, kw_hbm, vw_hbm, go_hbm,
    qg_ref, lg_ref, rg_ref, kg_ref, vg_ref,
    q_in, kw, vw, go, kv, kvt, bias, nope_s, qgl, pd,
    wbuf, wsib, wsum, wrecv, lbuf, lsib, lsum, lrecv, zbuf, zrecv, zout,
    in_sem, g_send, g_recv, ws_send, ws_recv, wc_send, wc_recv,
    ls_send, ls_recv, lc_send, lc_recv, zr_send, zr_recv, zg_send, zg_recv,
):
    T = lat_ref.shape[0]
    N = n * T
    C = n // 2
    pairs = kw.shape[1] // (2 * NOPE)
    nb = D_LATENT // n
    G = order_ref.shape[0]
    glen = N // G
    R = T // nz
    scale = (NOPE + ROPE) ** -0.5

    me = lax.axis_index("ctx")
    z = lax.axis_index("head")
    core = lax.rem(me, 2)
    chip = me // 2
    other = 1 - core
    sibling = chip * 2 + other

    def peer(r):
        return lax.rem(chip + r, C) * 2 + core

    def ahead(r):
        return lax.rem(z + r, nz)

    loads = [
        pltpu.make_async_copy(src, dst, in_sem.at[i])
        for i, (src, dst) in enumerate(
            ((q_hbm, q_in), (kw_hbm, kw), (go_hbm, go), (vw_hbm, vw))
        )
    ]
    for load in loads:
        load.start()

    barrier = pltpu.get_barrier_semaphore()
    pl.semaphore_signal(barrier, inc=1, device_id={"ctx": sibling}, device_id_type=MESH)
    for r in range(1, C):
        pl.semaphore_signal(barrier, inc=1, device_id={"ctx": peer(r)}, device_id_type=MESH)
    for r in range(1, nz):
        pl.semaphore_signal(barrier, inc=1, device_id={"head": ahead(r)}, device_id_type=MESH)

    own = pl.ds(pl.multiple_of(me * T, T), T)
    kv[own, :D_LATENT] = lat_ref[...]
    kv[own, D_LATENT:] = jnp.concatenate([rope_ref[...], jnp.zeros((T, WIDE - D_LATENT - ROPE), BF16)], axis=1)
    pl.semaphore_wait(barrier, 1 + (C - 1) + (nz - 1))

    def send(src, dst, s_sem, r_sem, where):
        return pltpu.make_async_remote_copy(
            src_ref=src, dst_ref=dst, send_sem=s_sem, recv_sem=r_sem,
            device_id=where, device_id_type=MESH,
        )

    gathers = []
    for r in range(1, C):
        cp = send(kv.at[own], kv.at[own], g_send.at[r], g_recv.at[r], {"ctx": peer(r)})
        cp.start()
        gathers.append(cp)
    to_sib = send(kv.at[own], kv.at[own], g_send.at[0], g_recv.at[0], {"ctx": sibling})
    to_sib.start()

    lane = lax.broadcasted_iota(jnp.int32, (1, T), 1)
    qpos = jnp.zeros((1, T), jnp.int32)
    for k in range(T // glen):
        base = order_ref[me * (T // glen) + k] * glen - k * glen
        qpos = jnp.where(lane // glen == k, base + lane, qpos)
    row = lax.broadcasted_iota(jnp.int32, (glen, T), 0)

    def fill_bias(g, carry):
        kpos = order_ref[g] * glen + row
        bias[pl.ds(pl.multiple_of(g * glen, glen), glen), :] = jnp.where(kpos <= qpos, 0.0, NEG_FILL)
        return carry

    lax.fori_loop(0, G, fill_bias, 0)
    for load in loads:
        load.wait()

    def prepare(p, carry):
        x = q_in[:, pl.ds(pl.multiple_of(p * 384, 128), 384)].astype(F32)
        for hh in range(2):
            cols = pl.ds(pl.multiple_of(p * 256 + hh * 128, 128), 128)
            nope = x[:, hh * 192:hh * 192 + 128].astype(BF16)
            rp = x[:, hh * 192 + 128:hh * 192 + 192]
            nope_s[p, hh * T:(hh + 1) * T, :] = nope
            top = pl.ds(pl.multiple_of(p * 4 * T + hh * T, T), T)
            low = pl.ds(pl.multiple_of(p * 4 * T + (2 + hh) * T, T), T)
            qgl[top, :D_LATENT] = dot(nope, kw[:, cols], 1, 1).astype(BF16)
            qgl[top, D_LATENT:] = jnp.concatenate([rp, jnp.zeros((T, 64), F32)], axis=1).astype(BF16)
            qgl[low, :D_LATENT] = dot(go[:, cols], vw[:, cols], 1, 1).astype(BF16)
            qgl[low, D_LATENT:] = jnp.zeros((T, WIDE - D_LATENT), BF16)
        return carry

    lax.fori_loop(0, pairs, prepare, 0)

    forwards = []
    for r in range(1, C):
        gathers[r - 1].wait_recv()
        block = lax.rem(chip - r + C, C) * 2 + core
        rows = pl.ds(pl.multiple_of(block * T, T), T)
        cp = send(kv.at[rows], kv.at[rows], g_send.at[C - 1 + r], g_recv.at[C - 1 + r], {"ctx": sibling})
        cp.start()
        forwards.append(cp)
    to_sib.wait_recv()
    for cp in forwards:
        cp.wait_recv()

    def flip(b, carry):
        rows = pl.ds(pl.multiple_of(b * T, T), T)
        kvt[:, rows] = kv[rows, :].T
        return carry

    lax.fori_loop(0, n, flip, 0)

    def w_sib(p):
        return send(wbuf.at[p, other], wsib.at[p], ws_send.at[p], ws_recv.at[p], {"ctx": sibling})

    def w_chip(p, r):
        to = lax.rem(chip + r, C)
        rows = pl.ds(pl.multiple_of(to * nb, nb), nb)
        return send(
            wsum.at[p, rows], wrecv.at[p, r - 1],
            wc_send.at[p, r - 1], wc_recv.at[p, r - 1], {"ctx": to * 2 + core},
        )

    def w_pass(p):
        w_sib(p).wait_recv()
        wsum[p] = (wbuf[p, core].astype(F32) + wsib[p].astype(F32)).astype(BF16)
        for r in range(1, C):
            w_chip(p, r).start()

    def pair(p, carry):
        q = qgl[pl.ds(pl.multiple_of(p * 4 * T, T), 2 * T), :]
        gl = qgl[pl.ds(pl.multiple_of(p * 4 * T + 2 * T, T), 2 * T), :D_LATENT]
        b1 = bias[...]
        s = dot(kv[...], q, 1, 1) * scale + jnp.concatenate([b1, b1], axis=1)
        g = dot(kv[:, :D_LATENT], gl, 1, 1)
        top = jnp.max(s, axis=0, keepdims=True)
        e = jnp.exp(s - top)
        inv = 1.0 / jnp.sum(e, axis=0, keepdims=True)
        delta = jnp.sum(e * g, axis=0, keepdims=True) * inv
        pr = e * inv
        ds = (pr * (g - delta) * scale).astype(BF16)
        pr = pr.astype(BF16)
        base = p * 4 * T
        pd[:, pl.ds(pl.multiple_of(base, T), 2 * T)] = ds
        pd[:, pl.ds(pl.multiple_of(base + 2 * T, T), 2 * T)] = pr
        got = dot(kvt[...], ds)
        ga = got[:D_LATENT].astype(BF16)
        ol = dot(kvt[:D_LATENT, :], pr).astype(BF16)
        rg = got[D_LATENT:].T
        parts = []
        for hh in range(2):
            cols = pl.ds(pl.multiple_of(p * 256 + hh * 128, 128), 128)
            gah = ga[:, hh * T:(hh + 1) * T]
            wk = dot(gah, nope_s[p, hh * T:(hh + 1) * T, :]).astype(BF16)
            wv = dot(ol[:, hh * T:(hh + 1) * T], go[:, cols]).astype(BF16)
            for c in range(C):
                for j in range(2):
                    d = 2 * c + j
                    wbuf[p, j, c * nb:(c + 1) * nb, hh * 128:(hh + 1) * 128] = wk[d * nb:(d + 1) * nb]
                    wbuf[p, j, c * nb:(c + 1) * nb, 256 + hh * 128:256 + (hh + 1) * 128] = wv[d * nb:(d + 1) * nb]
            parts.append((gah, cols))
        w_sib(p).start()
        pieces = []
        for hh, (gah, cols) in enumerate(parts):
            pieces.append(dot(gah, kw[:, cols], 0, 0))
            pieces.append(rg[hh * T:(hh + 1) * T, :ROPE])
        qg_ref[:, pl.ds(pl.multiple_of(p * 384, 128), 384)] = jnp.concatenate(pieces, axis=1).astype(BF16)

        @pl.when(p >= 1)
        def _():
            w_pass(p - 1)

        return carry

    lax.fori_loop(0, pairs, pair, 0)

    def l_sib(i):
        return send(lbuf.at[i, other], lsib.at[i], ls_send.at[i], ls_recv.at[i], {"ctx": sibling})

    def l_chip(i):
        to = lax.rem(chip + 1 + i, C) * 2 + core
        return send(lsum.at[i], lrecv.at[i], lc_send.at[i], lc_recv.at[i], {"ctx": to})

    def l_pass(i):
        l_sib(i).wait_recv()
        lsum[i] = (lbuf[i, core].astype(F32) + lsib[i].astype(F32)).astype(BF16)
        l_chip(i).start()

    def keys(i, carry):
        to = lax.rem(chip + 1 + i, C)
        part = dot(pd[pl.ds(pl.multiple_of(to * 2 * T, 2 * T), 2 * T), :], qgl[...]).astype(BF16)
        lbuf[i, 0] = part[:T]
        lbuf[i, 1] = part[T:]
        l_sib(i).start()

        @pl.when(i == 0)
        def _():
            w_pass(pairs - 1)

        @pl.when(i >= 1)
        def _():
            l_pass(i - 1)

        return carry

    lax.fori_loop(0, C, keys, 0)

    l_sib(C - 1).wait_recv()
    total = lbuf[C - 1, core].astype(F32) + lsib[C - 1].astype(F32)
    for i in range(C - 1):
        l_chip(i).wait_recv()
        total = total + lrecv[i].astype(F32)
    zbuf[...] = total.astype(BF16)

    def z_add(r):
        rows = pl.ds(pl.multiple_of(ahead(r) * R, R), R)
        return send(zbuf.at[rows], zrecv.at[r - 1], zr_send.at[r - 1], zr_recv.at[r - 1], {"head": ahead(r)})

    for r in range(1, nz):
        z_add(r).start()

    def w_end(p, carry):
        rows = pl.ds(pl.multiple_of(chip * nb, nb), nb)
        acc = wsum[p, rows, :].astype(F32)
        for r in range(1, C):
            w_chip(p, r).wait_recv()
            acc = acc + wrecv[p, r - 1].astype(F32)
        cols = pl.ds(pl.multiple_of(p * 256, 256), 256)
        kg_ref[:, cols] = acc[:, :256]
        vg_ref[:, cols] = acc[:, 256:]
        return carry

    lax.fori_loop(0, pairs - 1, w_end, 0)

    mine = pl.ds(pl.multiple_of(z * R, R), R)
    acc = zbuf[mine, :].astype(F32)
    for r in range(1, nz):
        z_add(r).wait_recv()
        acc = acc + zrecv[r - 1].astype(F32)
    zout[mine, :] = acc.astype(BF16)

    def z_all(r):
        return send(zout.at[mine], zout.at[mine], zg_send.at[r - 1], zg_recv.at[r - 1], {"head": ahead(r)})

    for r in range(1, nz):
        z_all(r).start()
    w_end(pairs - 1, 0)

    for cp in gathers + forwards + [to_sib]:
        cp.wait_send()

    def w_sent(p, carry):
        w_sib(p).wait_send()
        for r in range(1, C):
            w_chip(p, r).wait_send()
        return carry

    lax.fori_loop(0, pairs, w_sent, 0)
    for i in range(C):
        l_sib(i).wait_send()
        if i < C - 1:
            l_chip(i).wait_send()
    for r in range(1, nz):
        z_add(r).wait_send()
        z_all(r).wait()
    lg_ref[...] = zout[:, :D_LATENT].astype(F32)
    rg_ref[...] = zout[:, D_LATENT:].astype(F32)[:, :ROPE]


def per_device(n, nz, queries, latents, rope_key, up_key_weight, up_value_weight, out_grad, group_order):
    T = queries.shape[0]
    width = up_key_weight.shape[1]
    N, C, pairs, nb, R = n * T, n // 2, width // 256, D_LATENT // n, T // nz
    vm = pl.BlockSpec(memory_space=pltpu.VMEM)
    hbm = pl.BlockSpec(memory_space=pl.ANY)
    dma = pltpu.SemaphoreType.DMA

    def buf(*shape, dtype=BF16):
        return pltpu.VMEM(shape, dtype)

    flops = 2 * 2 * pairs * T * N * (3 * WIDE + 3 * D_LATENT)
    return pl.pallas_call(
        functools.partial(kernel, n, nz),
        out_shape=(
            jax.ShapeDtypeStruct(queries.shape, BF16),
            jax.ShapeDtypeStruct((T, D_LATENT), F32),
            jax.ShapeDtypeStruct((T, ROPE), F32),
            jax.ShapeDtypeStruct((nb, width), F32),
            jax.ShapeDtypeStruct((nb, width), F32),
        ),
        in_specs=[vm, vm, pl.BlockSpec(memory_space=pltpu.SMEM), hbm, hbm, hbm, hbm],
        out_specs=(vm,) * 5,
        scratch_shapes=[
            buf(*queries.shape), buf(*up_key_weight.shape), buf(*up_value_weight.shape), buf(*out_grad.shape),
            buf(N, WIDE), buf(WIDE, N), buf(N, T, dtype=F32), buf(pairs, 2 * T, NOPE),
            buf(pairs * 4 * T, WIDE), buf(N, pairs * 4 * T),
            buf(pairs, 2, C * nb, 512), buf(pairs, C * nb, 512), buf(pairs, C * nb, 512),
            buf(pairs, C - 1, nb, 512),
            buf(C, 2, T, WIDE), buf(C, T, WIDE), buf(C - 1, T, WIDE), buf(C - 1, T, WIDE),
            buf(T, WIDE), buf(nz - 1, R, WIDE), buf(T, WIDE),
            dma((4,)), dma((2 * C - 1,)), dma((2 * C - 1,)),
            dma((pairs,)), dma((pairs,)), dma((pairs, C - 1)), dma((pairs, C - 1)),
            dma((C,)), dma((C,)), dma((C - 1,)), dma((C - 1,)),
            dma((nz - 1,)), dma((nz - 1,)), dma((nz - 1,)), dma((nz - 1,)),
        ],
        compiler_params=pltpu.CompilerParams(
            collective_id=0, has_side_effects=True, vmem_limit_bytes=60 * 1024 * 1024
        ),
        cost_estimate=pl.CostEstimate(flops=flops, bytes_accessed=8 * 1024 * 1024, transcendentals=2 * pairs * T * N),
        name="mla_backward",
    )(latents, rope_key, group_order, queries, up_key_weight, up_value_weight, out_grad)


def solution(mesh):
    placed = (
        P("ctx", "head"),
        P("ctx", None),
        P("ctx", None),
        P(None, "head"),
        P(None, "head"),
        P("ctx", "head"),
        P(),
    )
    return jax.shard_map(
        functools.partial(per_device, mesh.shape["ctx"], mesh.shape["head"]),
        mesh=mesh,
        in_specs=placed,
        out_specs=(
            P("ctx", "head"),
            P("ctx", None),
            P("ctx", None),
            P("ctx", "head"),
            P("ctx", "head"),
        ),
        check_vma=False,
    )
```

```python
import functools

import jax
import jax.numpy as jnp
from jax import lax
from jax.experimental import pallas as pl
from jax.experimental.pallas import tpu as pltpu
from jax.sharding import PartitionSpec as P

D_LATENT = 512
ROPE = 64
NOPE = 128
VDIM = 128
WIDE = 640

NEG_FILL = -1e30
MESH = pl.DeviceIdType.MESH
F32 = jnp.float32
BF16 = jnp.bfloat16


def dot(a, b, ca=1, cb=0):
    return lax.dot_general(a, b, (((ca,), (cb,)), ((), ())), preferred_element_type=F32)


def kernel(
    n, nz, lat_ref, rope_ref, order_ref, q_hbm, kw_hbm, vw_hbm, go_hbm,
    qg_ref, lg_ref, rg_ref, kg_ref, vg_ref,
    q_in, kw, vw, go, kv, kvt, bias, nope_s, qgl, pd,
    wbuf, wsib, wsum, wrecv, lbuf, lsib, lsum, lrecv, zbuf, zrecv, zout,
    in_sem, g_send, g_recv, ws_send, ws_recv, wc_send, wc_recv,
    ls_send, ls_recv, lc_send, lc_recv, zr_send, zr_recv, zg_send, zg_recv,
):
    T = lat_ref.shape[0]
    N = n * T
    C = n // 2
    pairs = kw.shape[1] // (2 * NOPE)
    nb = D_LATENT // n
    G = order_ref.shape[0]
    glen = N // G
    R = T // nz
    scale = (NOPE + ROPE) ** -0.5

    me = lax.axis_index("ctx")
    z = lax.axis_index("head")
    core = lax.rem(me, 2)
    chip = me // 2
    other = 1 - core
    sibling = chip * 2 + other

    def peer(r):
        return lax.rem(chip + r, C) * 2 + core

    def ahead(r):
        return lax.rem(z + r, nz)

    loads = [
        pltpu.make_async_copy(src, dst, in_sem.at[i])
        for i, (src, dst) in enumerate(
            ((q_hbm, q_in), (kw_hbm, kw), (go_hbm, go), (vw_hbm, vw))
        )
    ]
    for load in loads:
        load.start()

    barrier = pltpu.get_barrier_semaphore()
    pl.semaphore_signal(barrier, inc=1, device_id={"ctx": sibling}, device_id_type=MESH)
    for r in range(1, C):
        pl.semaphore_signal(barrier, inc=1, device_id={"ctx": peer(r)}, device_id_type=MESH)
    for r in range(1, nz):
        pl.semaphore_signal(barrier, inc=1, device_id={"head": ahead(r)}, device_id_type=MESH)

    own = pl.ds(pl.multiple_of(me * T, T), T)
    kv[own, :D_LATENT] = lat_ref[...]
    kv[own, D_LATENT:] = jnp.concatenate(
        [rope_ref[...], jnp.zeros((WIDE - D_LATENT - ROPE, T), BF16)], axis=0
    ).T
    pl.semaphore_wait(barrier, 1 + (C - 1) + (nz - 1))

    def send(src, dst, s_sem, r_sem, where):
        return pltpu.make_async_remote_copy(
            src_ref=src, dst_ref=dst, send_sem=s_sem, recv_sem=r_sem,
            device_id=where, device_id_type=MESH,
        )

    gathers = []
    for r in range(1, C):
        cp = send(kv.at[own], kv.at[own], g_send.at[r], g_recv.at[r], {"ctx": peer(r)})
        cp.start()
        gathers.append(cp)
    to_sib = send(kv.at[own], kv.at[own], g_send.at[0], g_recv.at[0], {"ctx": sibling})
    to_sib.start()

    lane = lax.broadcasted_iota(jnp.int32, (1, T), 1)
    qpos = jnp.zeros((1, T), jnp.int32)
    for k in range(T // glen):
        base = order_ref[me * (T // glen) + k] * glen - k * glen
        qpos = jnp.where(lane // glen == k, base + lane, qpos)
    row = lax.broadcasted_iota(jnp.int32, (glen, T), 0)

    def fill_bias(g, carry):
        kpos = order_ref[g] * glen + row
        bias[pl.ds(pl.multiple_of(g * glen, glen), glen), :] = jnp.where(kpos <= qpos, 0.0, NEG_FILL)
        return carry

    lax.fori_loop(0, G, fill_bias, 0)
    for load in loads:
        load.wait()

    def prepare(p, carry):
        x = q_in[:, pl.ds(pl.multiple_of(p * 384, 128), 384)].astype(F32)
        for hh in range(2):
            cols = pl.ds(pl.multiple_of(p * 256 + hh * 128, 128), 128)
            nope = x[:, hh * 192:hh * 192 + 128].astype(BF16)
            rp = x[:, hh * 192 + 128:hh * 192 + 192]
            nope_s[p, hh * T:(hh + 1) * T, :] = nope
            top = pl.ds(pl.multiple_of(p * 4 * T + hh * T, T), T)
            low = pl.ds(pl.multiple_of(p * 4 * T + (2 + hh) * T, T), T)
            qgl[top, :D_LATENT] = dot(nope, kw[:, cols], 1, 1).astype(BF16)
            qgl[top, D_LATENT:] = jnp.concatenate([rp, jnp.zeros((T, 64), F32)], axis=1).astype(BF16)
            qgl[low, :D_LATENT] = dot(go[:, cols], vw[:, cols], 1, 1).astype(BF16)
            qgl[low, D_LATENT:] = jnp.zeros((T, WIDE - D_LATENT), BF16)
        return carry

    lax.fori_loop(0, pairs, prepare, 0)

    def flip(b):
        rows = pl.ds(pl.multiple_of(b * T, T), T)
        kvt[:, rows] = kv[rows, :].T

    flip(me)
    forwards = []
    for r in range(1, C):
        gathers[r - 1].wait_recv()
        block = lax.rem(chip - r + C, C) * 2 + core
        rows = pl.ds(pl.multiple_of(block * T, T), T)
        cp = send(kv.at[rows], kv.at[rows], g_send.at[C - 1 + r], g_recv.at[C - 1 + r], {"ctx": sibling})
        cp.start()
        forwards.append(cp)
        flip(block)
    to_sib.wait_recv()
    flip(sibling)
    for r in range(1, C):
        forwards[r - 1].wait_recv()
        flip(lax.rem(chip - r + C, C) * 2 + other)

    def w_sib(p):
        return send(wbuf.at[p, other], wsib.at[p], ws_send.at[p], ws_recv.at[p], {"ctx": sibling})

    def w_chip(p, r):
        to = lax.rem(chip + r, C)
        rows = pl.ds(pl.multiple_of(to * nb, nb), nb)
        return send(
            wsum.at[p, rows], wrecv.at[p, r - 1],
            wc_send.at[p, r - 1], wc_recv.at[p, r - 1], {"ctx": to * 2 + core},
        )

    def w_pass(p):
        w_sib(p).wait_recv()
        wsum[p] = (wbuf[p, core].astype(F32) + wsib[p].astype(F32)).astype(BF16)
        for r in range(1, C):
            w_chip(p, r).start()

    def pair(p, carry):
        q = qgl[pl.ds(pl.multiple_of(p * 4 * T, T), 2 * T), :]
        gl = qgl[pl.ds(pl.multiple_of(p * 4 * T + 2 * T, T), 2 * T), :D_LATENT]
        b1 = bias[...]
        s = dot(kv[...], q, 1, 1) * scale + jnp.concatenate([b1, b1], axis=1)
        g = dot(kv[:, :D_LATENT], gl, 1, 1)
        top = jnp.max(s, axis=0, keepdims=True)
        e = jnp.exp(s - top)
        inv = 1.0 / jnp.sum(e, axis=0, keepdims=True)
        delta = jnp.sum(e * g, axis=0, keepdims=True) * inv
        pr = e * inv
        ds = (pr * (g - delta) * scale).astype(BF16)
        pr = pr.astype(BF16)
        base = p * 4 * T
        pd[:, pl.ds(pl.multiple_of(base, T), 2 * T)] = ds
        pd[:, pl.ds(pl.multiple_of(base + 2 * T, T), 2 * T)] = pr
        got = dot(kvt[...], ds)
        ga = got[:D_LATENT].astype(BF16)
        ol = dot(kvt[:D_LATENT, :], pr).astype(BF16)
        rg = got[D_LATENT:].T
        parts = []
        for hh in range(2):
            cols = pl.ds(pl.multiple_of(p * 256 + hh * 128, 128), 128)
            gah = ga[:, hh * T:(hh + 1) * T]
            wk = dot(gah, nope_s[p, hh * T:(hh + 1) * T, :]).astype(BF16)
            wv = dot(ol[:, hh * T:(hh + 1) * T], go[:, cols]).astype(BF16)
            for c in range(C):
                for j in range(2):
                    d = 2 * c + j
                    wbuf[p, j, c * nb:(c + 1) * nb, hh * 128:(hh + 1) * 128] = wk[d * nb:(d + 1) * nb]
                    wbuf[p, j, c * nb:(c + 1) * nb, 256 + hh * 128:256 + (hh + 1) * 128] = wv[d * nb:(d + 1) * nb]
            parts.append((gah, cols))
        w_sib(p).start()
        pieces = []
        for hh, (gah, cols) in enumerate(parts):
            pieces.append(dot(gah, kw[:, cols], 0, 0))
            pieces.append(rg[hh * T:(hh + 1) * T, :ROPE])
        qg_ref[:, pl.ds(pl.multiple_of(p * 384, 128), 384)] = jnp.concatenate(pieces, axis=1).astype(BF16)

        @pl.when(p >= 1)
        def _():
            w_pass(p - 1)

        return carry

    lax.fori_loop(0, pairs, pair, 0)

    def l_sib(i):
        return send(lbuf.at[i, other], lsib.at[i], ls_send.at[i], ls_recv.at[i], {"ctx": sibling})

    def l_chip(i):
        to = lax.rem(chip + 1 + i, C) * 2 + core
        return send(lsum.at[i], lrecv.at[i], lc_send.at[i], lc_recv.at[i], {"ctx": to})

    def l_pass(i):
        l_sib(i).wait_recv()
        lsum[i] = (lbuf[i, core].astype(F32) + lsib[i].astype(F32)).astype(BF16)
        l_chip(i).start()

    def keys(i, carry):
        to = lax.rem(chip + 1 + i, C)
        part = dot(pd[pl.ds(pl.multiple_of(to * 2 * T, 2 * T), 2 * T), :], qgl[...]).astype(BF16)
        lbuf[i, 0] = part[:T]
        lbuf[i, 1] = part[T:]
        l_sib(i).start()

        @pl.when(i == 0)
        def _():
            w_pass(pairs - 1)

        @pl.when(i >= 1)
        def _():
            l_pass(i - 1)

        return carry

    lax.fori_loop(0, C, keys, 0)

    l_sib(C - 1).wait_recv()
    total = lbuf[C - 1, core].astype(F32) + lsib[C - 1].astype(F32)
    for i in range(C - 1):
        l_chip(i).wait_recv()
        total = total + lrecv[i].astype(F32)
    zbuf[...] = total.astype(BF16)

    def z_add(r):
        rows = pl.ds(pl.multiple_of(ahead(r) * R, R), R)
        return send(zbuf.at[rows], zrecv.at[r - 1], zr_send.at[r - 1], zr_recv.at[r - 1], {"head": ahead(r)})

    for r in range(1, nz):
        z_add(r).start()

    def w_end(p, carry):
        rows = pl.ds(pl.multiple_of(chip * nb, nb), nb)
        acc = wsum[p, rows, :].astype(F32)
        for r in range(1, C):
            w_chip(p, r).wait_recv()
            acc = acc + wrecv[p, r - 1].astype(F32)
        cols = pl.ds(pl.multiple_of(p * 256, 256), 256)
        kg_ref[:, cols] = acc[:, :256]
        vg_ref[:, cols] = acc[:, 256:]
        return carry

    lax.fori_loop(0, pairs - 1, w_end, 0)

    mine = pl.ds(pl.multiple_of(z * R, R), R)
    acc = zbuf[mine, :].astype(F32)
    for r in range(1, nz):
        z_add(r).wait_recv()
        acc = acc + zrecv[r - 1].astype(F32)
    zout[mine, :] = acc.astype(BF16)

    def z_all(r):
        return send(zout.at[mine], zout.at[mine], zg_send.at[r - 1], zg_recv.at[r - 1], {"head": ahead(r)})

    for r in range(1, nz):
        z_all(r).start()
    w_end(pairs - 1, 0)

    for cp in gathers + forwards + [to_sib]:
        cp.wait_send()

    def w_sent(p, carry):
        w_sib(p).wait_send()
        for r in range(1, C):
            w_chip(p, r).wait_send()
        return carry

    lax.fori_loop(0, pairs, w_sent, 0)
    for i in range(C):
        l_sib(i).wait_send()
        if i < C - 1:
            l_chip(i).wait_send()
    for r in range(1, nz):
        z_add(r).wait_send()
        z_all(r).wait()
    lg_ref[...] = zout[:, :D_LATENT].astype(F32)
    rg_ref[...] = zout[:, D_LATENT:].astype(F32).T[:ROPE]


def hand_over(*refs):
    src, dst, held, (into, out) = refs[:5], refs[5:10], refs[10:15], refs[15:]
    reads = [pltpu.make_async_copy(src[i], held[i], into.at[i]) for i in range(5)]
    writes = [pltpu.make_async_copy(held[i], dst[i], out.at[i]) for i in range(5)]
    for cp in reads:
        cp.start()
    for read, write in zip(reads, writes):
        read.wait()
        write.start()
    for cp in writes:
        cp.wait()


def per_device(n, nz, queries, latents, rope_key, up_key_weight, up_value_weight, out_grad, group_order):
    T = queries.shape[0]
    width = up_key_weight.shape[1]
    N, C, pairs, nb, R = n * T, n // 2, width // 256, D_LATENT // n, T // nz
    vm = pl.BlockSpec(memory_space=pltpu.VMEM)
    hbm = pl.BlockSpec(memory_space=pl.ANY)
    dma = pltpu.SemaphoreType.DMA

    def buf(*shape, dtype=BF16):
        return pltpu.VMEM(shape, dtype)

    flops = 2 * 2 * pairs * T * N * (3 * WIDE + 3 * D_LATENT)
    results = pl.pallas_call(
        functools.partial(kernel, n, nz),
        out_shape=(
            jax.ShapeDtypeStruct(queries.shape, BF16),
            jax.ShapeDtypeStruct((T, D_LATENT), F32),
            jax.ShapeDtypeStruct((ROPE, T), F32),
            jax.ShapeDtypeStruct((nb, width), F32),
            jax.ShapeDtypeStruct((nb, width), F32),
        ),
        in_specs=[vm, vm, pl.BlockSpec(memory_space=pltpu.SMEM), hbm, hbm, hbm, hbm],
        out_specs=(vm,) * 5,
        scratch_shapes=[
            buf(*queries.shape), buf(*up_key_weight.shape), buf(*up_value_weight.shape), buf(*out_grad.shape),
            buf(N, WIDE), buf(WIDE, N), buf(N, T, dtype=F32), buf(pairs, 2 * T, NOPE),
            buf(pairs * 4 * T, WIDE), buf(N, pairs * 4 * T),
            buf(pairs, 2, C * nb, 512), buf(pairs, C * nb, 512), buf(pairs, C * nb, 512),
            buf(pairs, C - 1, nb, 512),
            buf(C, 2, T, WIDE), buf(C, T, WIDE), buf(C - 1, T, WIDE), buf(C - 1, T, WIDE),
            buf(T, WIDE), buf(nz - 1, R, WIDE), buf(T, WIDE),
            dma((4,)), dma((2 * C - 1,)), dma((2 * C - 1,)),
            dma((pairs,)), dma((pairs,)), dma((pairs, C - 1)), dma((pairs, C - 1)),
            dma((C,)), dma((C,)), dma((C - 1,)), dma((C - 1,)),
            dma((nz - 1,)), dma((nz - 1,)), dma((nz - 1,)), dma((nz - 1,)),
        ],
        compiler_params=pltpu.CompilerParams(
            collective_id=0, has_side_effects=True, vmem_limit_bytes=60 * 1024 * 1024
        ),
        cost_estimate=pl.CostEstimate(flops=flops, bytes_accessed=8 * 1024 * 1024, transcendentals=2 * pairs * T * N),
        name="mla_backward",
    )(latents, rope_key.T, group_order, queries, up_key_weight, up_value_weight, out_grad)
    out = pl.pallas_call(
        hand_over,
        out_shape=tuple(jax.ShapeDtypeStruct(x.shape, x.dtype) for x in results),
        in_specs=[hbm] * 5,
        out_specs=(hbm,) * 5,
        scratch_shapes=[pltpu.VMEM(x.shape, x.dtype) for x in results] + [dma((5,)), dma((5,))],
        name="hand_over",
    )(*results)
    return (out[0], out[1], out[2].T, out[3], out[4])


def solution(mesh):
    placed = (
        P("ctx", "head"),
        P("ctx", None),
        P("ctx", None),
        P(None, "head"),
        P(None, "head"),
        P("ctx", "head"),
        P(),
    )
    return jax.shard_map(
        functools.partial(per_device, mesh.shape["ctx"], mesh.shape["head"]),
        mesh=mesh,
        in_specs=placed,
        out_specs=(
            P("ctx", "head"),
            P("ctx", None),
            P("ctx", None),
            P("ctx", "head"),
            P("ctx", "head"),
        ),
        check_vma=False,
    )
```
